512 devices in a mesh: rep: 64 (over y_hi, z, x), fsdp: 8 (over y_lo, core).
Axes of the slice: x: 4, y: 8 (y_hi: 2, y_lo: 4; y = y_hi * 4 + y_lo), z: 8, core: 2. Of those that a mesh axis runs over, the one named last changes fastest.
Arguments:
- tokens: bfloat16 [64, 1024, 8192], P('rep', 'fsdp'), may hold values from -6 to 6
- master: float32 [64, 3, 64, 8192], P('rep', None, None, 'fsdp'), may hold values from -4 to 4
- first_moment: float32 [64, 3, 64, 8192], P('rep', None, None, 'fsdp'), may hold values from -0.002 to 0.002
- second_moment: float32 [64, 3, 64, 8192], P('rep', None, None, 'fsdp'), may hold values from 3e-09 to 3e-08
- step_counter: int32 [1], replicated, may hold values from 1000 to 99999
Outputs:
- mixed: bfloat16 [64, 3, 64, 8192], P('rep', None, None, 'fsdp')
The draws below stay inside these ranges and needn't reach their ends.
All inputs are finite; a program needn't handle non-finite values.
Results may differ from the reference program's by a relative error of at most 0.0056.
The reference program's roundings to bfloat16 on the way count: a program that leaves them out, or rounds other values in their place, can miss the bound.
Values may be sent and summed in bfloat16 or wider, within the bound.
A program may use at most 64 MiB of HBM per device.

```python
import math
import jax
import jax.numpy as jnp
from jax import lax

D = 8192
HID = 64
TOK_REP = 1024
N_REP = 64


def level_of(key, dims, pieces, smallest, high):
    gain = 1.0
    for dim, parts in pieces:
        heights = jax.random.uniform(jax.random.fold_in(jax.random.fold_in(key, 6), dim), (parts,), jnp.float32, smallest / len(pieces), high / len(pieces))
        gain = gain * jnp.repeat(jnp.exp(heights), dims[dim] // parts).reshape((-1,) + (1,) * (len(dims) - 1 - dim))
    return gain


def centred(key, shape, scale, most, cuts=(), held_as=jnp.bfloat16):
    loudness = level_of(key, shape, cuts, -0.22, 0.18) if cuts else 1.0
    result = jax.random.normal(key, shape, jnp.float32) * scale * loudness
    return jnp.minimum(jnp.maximum(result, -most), most).astype(held_as)


def setup_inputs(seed: int = 0) -> dict:
    arg_keys = jax.random.split(jax.random.key(seed), 6)
    return {
        "tokens": centred(arg_keys[0], (N_REP, TOK_REP, D), 1.0, 6.0, ((0, 64), (1, 8))),
        "master": centred(arg_keys[1], (N_REP, 3, HID, D), 1.0, 4.0, ((0, 64), (3, 8)), jnp.float32),
        "first_moment": centred(arg_keys[2], (N_REP, 3, HID, D), 0.0003, 0.002, ((0, 64), (3, 8)), jnp.float32),
        "second_moment": jnp.clip(jnp.exp(math.log(2.999999892949745e-08) - 2.30258505 * jax.random.uniform(arg_keys[3], (N_REP, 3, HID, D), jnp.float32) ** level_of(arg_keys[3], (N_REP, 3, HID, D), ((0, 64), (3, 8)), -0.2, 0.2)), 3.000000026176508e-09, 2.999999892949745e-08),
        "step_counter": jax.random.randint(arg_keys[4], (1,), 1000, 100000).astype(jnp.int32),
    }


def silu_parts(pre):
    sig = jax.nn.sigmoid(pre)
    return (pre * sig, sig * (1.0 + pre * (1.0 - sig)))

def adamw_update(param, moment_old, square_old, grads, step_float):
    moment = 0.9 * moment_old + 0.1 * grads
    square = 0.999 * square_old + 0.001 * grads * grads
    moment_hat = moment / (1.0 - jnp.power(0.9, step_float))
    square_hat = square / (1.0 - jnp.power(0.999, step_float))
    return param - 0.05 * (moment_hat / (jnp.sqrt(square_hat) + 1e-08) + 0.1 * param)

def replica_update(token_rows, master_rep, moment_rep, square_rep, step_float):
    width = token_rows.shape[1]
    hidden_units = master_rep.shape[1]
    count = token_rows.shape[0]
    scale_in = width ** (-0.5)
    scale_hid = hidden_units ** (-0.5)
    weights = master_rep.astype(jnp.bfloat16)
    gate_pre = scale_in * jnp.dot(token_rows, weights[0].T, preferred_element_type=jnp.float32)
    up_pre = scale_in * jnp.dot(token_rows, weights[1].T, preferred_element_type=jnp.float32)
    activated, slope_act = silu_parts(gate_pre)
    hidden = (activated * up_pre).astype(jnp.bfloat16)
    output = token_rows.astype(jnp.float32) + scale_hid * jnp.dot(hidden, weights[2], preferred_element_type=jnp.float32)
    cotangent = (output / count).astype(jnp.bfloat16)
    dhidden = scale_hid * jnp.dot(cotangent, weights[2].T, preferred_element_type=jnp.float32)
    dgate = (dhidden * up_pre * slope_act).astype(jnp.bfloat16)
    dup = (dhidden * activated).astype(jnp.bfloat16)
    grad_gate = scale_in * jnp.dot(dgate.T, token_rows, preferred_element_type=jnp.float32)
    grad_up = scale_in * jnp.dot(dup.T, token_rows, preferred_element_type=jnp.float32)
    grad_down = scale_hid * jnp.dot(hidden.T, cotangent, preferred_element_type=jnp.float32)
    grads = jnp.stack([grad_gate, grad_up, grad_down])
    updated = adamw_update(master_rep, moment_rep, square_rep, grads, step_float)
    return updated.astype(jnp.bfloat16)

def reference(tokens, master, first_moment, second_moment, step_counter):
    step_float = step_counter[0].astype(jnp.float32) + 1.0
    shards = lax.map(lambda items: replica_update(items[0], items[1], items[2], items[3], step_float), (tokens, master, first_moment, second_moment))
    bit_count = min(5, N_REP.bit_length() - 1)
    which_bit = (step_counter[0] % bit_count).astype(jnp.int32)
    partner = jnp.arange(N_REP, dtype=jnp.int32) ^ jnp.left_shift(jnp.int32(1), which_bit)
    other = shards[partner]
    return (0.5 * (shards.astype(jnp.float32) + other.astype(jnp.float32))).astype(jnp.bfloat16)
```

```python
import functools
import math

import jax
import jax.numpy as jnp
from jax import lax
from jax.experimental import pallas as pl
from jax.experimental.pallas import tpu as pltpu
from jax.sharding import PartitionSpec as P

MESH = pl.DeviceIdType.MESH
F32 = jnp.float32
BF16 = jnp.bfloat16
NT = (((1,), (1,)), ((), ()))
ROWS = 64


def dot(a, b):
    return jnp.dot(a, b, preferred_element_type=F32)


def dot_nt(a, b):
    return lax.dot_general(a, b, NT, preferred_element_type=F32)


def split(x):
    hi = x.astype(BF16)
    return hi, (x - hi.astype(F32)).astype(BF16)


def kernel(
    bit, step, tokens, master, moment, square, out,
    tok, wts, acc, own, mom, sqr, part, part_in, fac, hth, mine, other,
    tok_sem, tok_send, tok_recv, mas_sem, opt_sem, w_send, w_recv, p_sem,
    g_send, g_recv, s_send, s_recv, o_sem,
):
    rep = lax.axis_index("rep")
    me = lax.axis_index("fsdp")
    hid = own.shape[1]
    cols = own.shape[2]
    rows = 3 * hid
    near = tok.shape[1] // 2
    chunks = rows // ROWS
    per = hid // ROWS
    width = cols * lax.axis_size("fsdp")
    tok_rep = near * lax.axis_size("fsdp")
    scale_in = float(width) ** -0.5
    scale_hid = float(hid) ** -0.5

    chip = me // 2
    core = me % 2
    low = chip < 2
    edge = jnp.logical_or(chip == 0, chip == 3)
    inner = jnp.logical_not(edge)
    way = jnp.where(low, 0, 1)
    back_way = 1 - way
    forward = jnp.where(low, me + 2, me - 2)
    backward = jnp.where(low, me - 2, me + 2)
    sibling = me + 1 - 2 * core
    mate = jnp.where((rep // 2**bit) % 2 == 0, rep + 2**bit, rep - 2**bit)

    def slot(j):
        return jnp.where(low, j, 3 - j)

    barrier = pltpu.get_barrier_semaphore()
    pl.semaphore_signal(barrier, inc=1, device_id=(rep, sibling), device_id_type=MESH)
    pl.semaphore_signal(barrier, inc=1, device_id=(rep, forward), device_id_type=MESH)
    pl.semaphore_signal(barrier, inc=1, device_id=(mate, me), device_id_type=MESH)

    @pl.when(inner)
    def _():
        pl.semaphore_signal(barrier, inc=1, device_id=(rep, backward), device_id_type=MESH)

    def span(a):
        return pl.ds(a * ROWS, ROWS)

    def inside(a):
        return pl.ds((a % per) * ROWS, ROWS)

    def mas_copy(a):
        return pltpu.make_async_copy(
            master.at[0, a // per, inside(a)], own.at[a // per, inside(a)], mas_sem.at[a]
        )

    for a in range(chunks):
        mas_copy(a).start()

    def tok_copy(j):
        return pltpu.make_async_copy(
            tokens.at[0, :, pl.ds(pl.multiple_of((2 * j + core) * cols, cols), cols)],
            tok.at[j, pl.ds(pl.multiple_of(core * near, near), near)],
            tok_sem.at[j],
        )

    def tok_remote(j):
        return pltpu.make_async_remote_copy(
            src_ref=tokens.at[0, :, pl.ds(pl.multiple_of((2 * j + 1 - core) * cols, cols), cols)],
            dst_ref=tok.at[j, pl.ds(pl.multiple_of(core * near, near), near)],
            send_sem=tok_send.at[j],
            recv_sem=tok_recv.at[j],
            device_id=(rep, sibling),
            device_id_type=MESH,
        )

    for j in range(4):
        tok_copy(j).start()
    mom_copy = pltpu.make_async_copy(moment.at[0], mom, opt_sem.at[0])
    sqr_copy = pltpu.make_async_copy(square.at[0], sqr, opt_sem.at[1])
    mom_copy.start()
    sqr_copy.start()

    @pl.when(edge)
    def _():
        pl.semaphore_wait(barrier, 3)

    @pl.when(inner)
    def _():
        pl.semaphore_wait(barrier, 4)

    def w_copy(j, a, to, which):
        return pltpu.make_async_remote_copy(
            src_ref=wts.at[j, span(a)],
            dst_ref=wts.at[j, span(a)],
            send_sem=w_send.at[which, j, a],
            recv_sem=w_recv.at[j, a],
            device_id=(rep, to),
            device_id_type=MESH,
        )

    def w_forward(j, a):
        return w_copy(j, a, forward, 0)

    def w_back(j, a):
        return w_copy(j, a, backward, 1)

    home = chip
    for a in range(chunks):
        mas_copy(a).wait()
        wts[home, span(a)] = own[a // per, inside(a)].astype(BF16)
        w_forward(home, a).start()

        @pl.when(inner)
        def _():
            w_back(home, a).start()

    for j in range(4):
        tok_remote(j).start()

    def project(j, a):
        part[span(a)] += dot_nt(wts[j, span(a)], tok[j])

    def gram(j):
        wj = wts[j, pl.ds(2 * hid, hid)]
        part[pl.ds(rows, hid), pl.ds(0, hid)] += dot_nt(wj, wj)

    part[...] = jnp.zeros_like(part)
    for j in range(4):
        tok_copy(j).wait()
        tok_remote(j).wait_recv()
    for a in range(chunks):
        project(home, a)
    gram(home)

    @pl.when(inner)
    def _():
        for a in range(chunks):
            w_forward(slot(0), a).wait_recv()
            w_forward(slot(0), a).start()
            w_forward(slot(2), a).wait_recv()
            w_back(slot(2), a).start()
            project(slot(0), a)
            project(slot(2), a)
        for a in range(chunks):
            w_forward(slot(3), a).wait_recv()
            w_back(slot(3), a).start()
            if a == 0:
                gram(slot(0))
                gram(slot(2))
            project(slot(3), a)
        gram(slot(3))

    @pl.when(edge)
    def _():
        for j in range(1, 4):
            for a in range(chunks):
                w_forward(slot(j), a).wait_recv()
                project(slot(j), a)
            gram(slot(j))

    swap = pltpu.make_async_remote_copy(
        src_ref=part,
        dst_ref=part_in,
        send_sem=p_sem.at[0],
        recv_sem=p_sem.at[1],
        device_id=(rep, sibling),
        device_id_type=MESH,
    )
    swap.start()
    swap.wait_recv()
    gate = scale_in * (part[0:hid] + part_in[0:hid])
    up = scale_in * (part[hid : 2 * hid] + part_in[hid : 2 * hid])
    down = part[2 * hid : rows] + part_in[2 * hid : rows]
    sig = jax.nn.sigmoid(gate)
    act = gate * sig
    hidden = (act * up).astype(BF16)
    wwt_hi, wwt_lo = split(part[rows:, 0:hid] + part_in[rows:, 0:hid])
    through = dot(wwt_hi, hidden) + dot(wwt_lo, hidden)
    dhidden = (scale_hid / tok_rep) * (down + scale_hid * through)
    fac[0:hid] = (dhidden * up * (sig * (1.0 + gate * (1.0 - sig)))).astype(BF16)
    fac[hid : 2 * hid] = (dhidden * act).astype(BF16)
    fac[2 * hid : rows] = hidden
    hth_hi, hth_lo = split(scale_hid * dot_nt(hidden, hidden))
    hth[0] = hth_hi
    hth[1] = hth_lo

    def gradient(j, a):
        g = dot(fac[span(a)], tok[j])
        if a // per == 2:
            wj = wts[j, pl.ds(2 * hid, hid)]
            g = g + dot(hth[0, inside(a)], wj) + dot(hth[1, inside(a)], wj)
        return g

    def g_copy(way, j, a, to):
        return pltpu.make_async_remote_copy(
            src_ref=acc.at[way, j, span(a)],
            dst_ref=acc.at[way, j, span(a)],
            send_sem=g_send.at[way, j, a],
            recv_sem=g_recv.at[way, j, a],
            device_id=(rep, to),
            device_id_type=MESH,
        )

    def relay(way, j, a, to):
        g_copy(way, j, a, to).wait_recv()
        acc[way, j, span(a)] = (gradient(j, a) + acc[way, j, span(a)].astype(F32)).astype(BF16)
        g_copy(way, j, a, to).start()

    t = jnp.full((8, 128), step[0].astype(F32) + 1.0, F32)
    fix1 = (1.0 / (1.0 - jnp.exp(t * math.log(0.9))))[0:1, 0:1]
    fix2 = (1.0 / (1.0 - jnp.exp(t * math.log(0.999))))[0:1, 0:1]

    def s_copy(a):
        return pltpu.make_async_remote_copy(
            src_ref=mine.at[a // per, inside(a)],
            dst_ref=other.at[a // per, inside(a)],
            send_sem=s_send.at[a],
            recv_sem=s_recv.at[a],
            device_id=(mate, me),
            device_id_type=MESH,
        )

    def update(a, total):
        g = total * (scale_in if a // per < 2 else scale_hid / tok_rep)
        param = own[a // per, inside(a)]
        m = (0.9 * mom[a // per, inside(a)] + 0.1 * g) * fix1
        v = (0.999 * sqr[a // per, inside(a)] + (0.001 * g) * g) * fix2
        new = param - 0.05 * (m / (jnp.sqrt(v) + 1e-8) + 0.1 * param)
        mine[a // per, inside(a)] = new.astype(BF16)
        s_copy(a).start()

    def o_copy(a):
        return pltpu.make_async_copy(
            other.at[a // per, inside(a)], out.at[0, a // per, inside(a)], o_sem.at[a]
        )

    def mix(a):
        s_copy(a).wait_recv()
        both = mine[a // per, inside(a)].astype(F32) + other[a // per, inside(a)].astype(F32)
        other[a // per, inside(a)] = (0.5 * both).astype(BF16)
        o_copy(a).start()

    @pl.when(edge)
    def _():
        for j in (3, 2, 1):
            for a in range(chunks):
                acc[way, slot(j), span(a)] = gradient(slot(j), a).astype(BF16)
                g_copy(way, slot(j), a, forward).start()
        mom_copy.wait()
        sqr_copy.wait()
        for a in range(chunks):
            g = gradient(home, a)
            g_copy(back_way, home, a, forward).wait_recv()
            update(a, g + acc[back_way, home, span(a)].astype(F32))
            if a > 0:
                mix(a - 1)
        mix(chunks - 1)

    @pl.when(inner)
    def _():
        for a in range(chunks):
            relay(way, slot(3), a, forward)
            if a > 0:
                relay(back_way, slot(0), a - 1, backward)
        for a in range(chunks):
            relay(way, slot(2), a, forward)
            if a == 0:
                relay(back_way, slot(0), chunks - 1, backward)
        mom_copy.wait()
        sqr_copy.wait()
        for a in range(chunks):
            g = gradient(home, a)
            g_copy(back_way, home, a, forward).wait_recv()
            g = g + acc[back_way, home, span(a)].astype(F32)
            g_copy(way, home, a, forward).wait_recv()
            update(a, g + acc[way, home, span(a)].astype(F32))
            if a > 0:
                mix(a - 1)
        mix(chunks - 1)

    swap.wait_send()
    for j in range(4):
        tok_remote(j).wait_send()
    for a in range(chunks):
        s_copy(a).wait_send()
        o_copy(a).wait()
        w_forward(home, a).wait_send()

    @pl.when(edge)
    def _():
        for j in (3, 2, 1):
            for a in range(chunks):
                g_copy(way, slot(j), a, forward).wait_send()

    @pl.when(inner)
    def _():
        for a in range(chunks):
            w_forward(slot(0), a).wait_send()
            for j in (1, 2, 3):
                w_back(slot(j), a).wait_send()
            g_copy(way, slot(3), a, forward).wait_send()
            g_copy(way, slot(2), a, forward).wait_send()
            g_copy(back_way, slot(0), a, backward).wait_send()


def step_with(bit, tokens, master, moment, square, step):
    near = tokens.shape[1]
    hid, cols = master.shape[2:]
    rows = 3 * hid
    chunks = rows // ROWS
    dma = pltpu.SemaphoreType.DMA
    anywhere = pl.BlockSpec(memory_space=pl.ANY)
    return pl.pallas_call(
        functools.partial(kernel, bit),
        out_shape=jax.ShapeDtypeStruct(master.shape, BF16),
        in_specs=[pl.BlockSpec(memory_space=pltpu.SMEM)] + [anywhere] * 4,
        out_specs=anywhere,
        scratch_shapes=[
            pltpu.VMEM((4, 2 * near, cols), BF16),
            pltpu.VMEM((4, rows, cols), BF16),
            pltpu.VMEM((2, 4, rows, cols), BF16),
            pltpu.VMEM((3, hid, cols), F32),
            pltpu.VMEM((3, hid, cols), F32),
            pltpu.VMEM((3, hid, cols), F32),
            pltpu.VMEM((4 * hid, 2 * near), F32),
            pltpu.VMEM((4 * hid, 2 * near), F32),
            pltpu.VMEM((rows, 2 * near), BF16),
            pltpu.VMEM((2, hid, hid), BF16),
            pltpu.VMEM((3, hid, cols), BF16),
            pltpu.VMEM((3, hid, cols), BF16),
            dma((4,)), dma((4,)), dma((4,)),
            dma((chunks,)), dma((2,)),
            dma((2, 4, chunks)), dma((4, chunks)), dma((2,)),
            dma((2, 4, chunks)), dma((2, 4, chunks)),
            dma((chunks,)), dma((chunks,)), dma((chunks,)),
        ],
        compiler_params=pltpu.CompilerParams(
            collective_id=bit, has_side_effects=True, vmem_limit_bytes=40 * 2**20
        ),
        name=f"step_bit{bit}",
    )(step, tokens, master, moment, square)


def per_device(tokens, master, first_moment, second_moment, step_counter):
    bit_count = min(5, lax.axis_size("rep").bit_length() - 1)
    branches = [functools.partial(step_with, bit) for bit in range(bit_count)]
    return lax.switch(
        step_counter[0] % bit_count,
        branches, tokens, master, first_moment, second_moment, step_counter,
    )


def solution(mesh):
    sharded = P("rep", None, None, "fsdp")
    return jax.shard_map(
        per_device,
        mesh=mesh,
        in_specs=(P("rep", "fsdp", None), sharded, sharded, sharded, P()),
        out_specs=sharded,
        check_vma=False,
    )
```

```python
import functools
import math

import jax
import jax.numpy as jnp
from jax import lax
from jax.experimental import pallas as pl
from jax.experimental.pallas import tpu as pltpu
from jax.sharding import PartitionSpec as P

MESH = pl.DeviceIdType.MESH
F32 = jnp.float32
BF16 = jnp.bfloat16
NT = (((1,), (1,)), ((), ()))
ROWS = 64


def dot(a, b):
    return jnp.dot(a, b, preferred_element_type=F32)


def dot_nt(a, b):
    return lax.dot_general(a, b, NT, preferred_element_type=F32)


def split(x):
    hi = x.astype(BF16)
    return hi, (x - hi.astype(F32)).astype(BF16)


def kernel(
    bit, step, tokens, master, moment, square, out,
    tok, wts, acc, own, mom, sqr, part, part_in, fac, mine, other,
    tok_sem, tok_send, tok_recv, mas_sem, opt_sem, w_send, w_recv, p_sem,
    g_send, g_recv, s_send, s_recv, o_sem,
):
    rep = lax.axis_index("rep")
    me = lax.axis_index("fsdp")
    hid = own.shape[0] // 3
    cols = own.shape[1]
    rows = 3 * hid
    near = tokens.shape[1]
    both = 2 * near
    chunks = rows // ROWS
    per = hid // ROWS
    width = cols * lax.axis_size("fsdp")
    tok_rep = near * lax.axis_size("fsdp")
    scale_in = float(width) ** -0.5
    scale_hid = float(hid) ** -0.5

    chip = me // 2
    core = me % 2
    low = chip < 2
    edge = jnp.logical_or(chip == 0, chip == 3)
    inner = jnp.logical_not(edge)
    way = jnp.where(low, 0, 1)
    forward = jnp.where(low, me + 2, me - 2)
    backward = jnp.where(low, me - 2, me + 2)
    sibling = me + 1 - 2 * core
    mate = jnp.where((rep // 2**bit) % 2 == 0, rep + 2**bit, rep - 2**bit)
    home = chip

    def slot(j):
        return jnp.where(low, j, 3 - j)

    def look(i, at_edge, at_inner):
        found = 0
        for n, (e, m) in enumerate(zip(at_edge, at_inner)):
            found = jnp.where(i == n, jnp.where(edge, e, m), found)
        return found

    barrier = pltpu.get_barrier_semaphore()
    pl.semaphore_signal(barrier, inc=1, device_id=(rep, sibling), device_id_type=MESH)
    pl.semaphore_signal(barrier, inc=1, device_id=(rep, forward), device_id_type=MESH)
    pl.semaphore_signal(barrier, inc=1, device_id=(mate, me), device_id_type=MESH)

    @pl.when(inner)
    def _():
        pl.semaphore_signal(barrier, inc=1, device_id=(rep, backward), device_id_type=MESH)

    def span(a):
        return pl.ds(pl.multiple_of(a * ROWS, ROWS), ROWS)

    def inside(a):
        return pl.ds(pl.multiple_of((a % per) * ROWS, ROWS), ROWS)

    def mas_copy(a):
        return pltpu.make_async_copy(
            master.at[0, a // per, inside(a)], own.at[span(a)], mas_sem.at[a]
        )

    def tok_copy(j):
        return pltpu.make_async_copy(
            tokens.at[0, :, pl.ds(pl.multiple_of((2 * j + core) * cols, cols), cols)],
            tok.at[j, pl.ds(pl.multiple_of(core * near, near), near)],
            tok_sem.at[j],
        )

    def tok_remote(j):
        return pltpu.make_async_remote_copy(
            src_ref=tokens.at[0, :, pl.ds(pl.multiple_of((2 * j + 1 - core) * cols, cols), cols)],
            dst_ref=tok.at[j, pl.ds(pl.multiple_of(core * near, near), near)],
            send_sem=tok_send.at[j],
            recv_sem=tok_recv.at[j],
            device_id=(rep, sibling),
            device_id_type=MESH,
        )

    def opt_copy(m):
        here = pl.ds(pl.multiple_of(m * hid, hid), hid)
        return (
            pltpu.make_async_copy(moment.at[0, m], mom.at[here], opt_sem.at[0, m]),
            pltpu.make_async_copy(square.at[0, m], sqr.at[here], opt_sem.at[1, m]),
        )

    def w_copy(j, a, to, which):
        return pltpu.make_async_remote_copy(
            src_ref=wts.at[j, span(a)],
            dst_ref=wts.at[j, span(a)],
            send_sem=w_send.at[which, j, a],
            recv_sem=w_recv.at[j, a],
            device_id=(rep, to),
            device_id_type=MESH,
        )

    def g_copy(d, j, a, to):
        return pltpu.make_async_remote_copy(
            src_ref=acc.at[d, j, span(a)],
            dst_ref=acc.at[d, j, span(a)],
            send_sem=g_send.at[d, j, a],
            recv_sem=g_recv.at[d, j, a],
            device_id=(rep, to),
            device_id_type=MESH,
        )

    def s_copy(a):
        return pltpu.make_async_remote_copy(
            src_ref=mine.at[span(a)],
            dst_ref=other.at[span(a)],
            send_sem=s_send.at[a],
            recv_sem=s_recv.at[a],
            device_id=(mate, me),
            device_id_type=MESH,
        )

    def o_copy(a):
        return pltpu.make_async_copy(
            other.at[span(a)], out.at[0, a // per, inside(a)], o_sem.at[a]
        )

    def each(count):
        def run(body):
            lax.fori_loop(0, count, lambda i, c: (body(i), c)[1], 0)

        return run

    @each(chunks)
    def _(a):
        mas_copy(a).start()

    @each(4)
    def _(j):
        tok_copy(j).start()

    @each(3)
    def _(m):
        for copy in opt_copy(m):
            copy.start()

    pl.semaphore_wait(barrier, jnp.where(edge, 3, 4))

    @each(chunks)
    def _(a):
        mas_copy(a).wait()
        wts[home, span(a)] = own[span(a)].astype(BF16)
        w_copy(home, a, forward, 0).start()

        @pl.when(inner)
        def _():
            w_copy(home, a, backward, 1).start()

    @each(4)
    def _(j):
        tok_remote(j).start()

    part[...] = jnp.zeros_like(part)
    fac[pl.ds(0, 2 * hid), pl.ds(both, 2 * hid)] = jnp.zeros((2 * hid, 2 * hid), BF16)

    @pl.when(edge)
    def _():
        @each(4)
        def _(j):
            acc[way, j] = jnp.zeros(acc.shape[2:], BF16)

    @each(4)
    def _(j):
        tok_copy(j).wait()
        tok_remote(j).wait_recv()

    @each(4 * chunks)
    def _(i):
        n = i - chunks
        first = i < chunks
        in_pair = n < 2 * chunks
        j_inner = jnp.where(in_pair, 2 * (n % 2), 3)
        a_inner = jnp.where(in_pair, n // 2, n - 2 * chunks)
        j_edge = 1 + n // chunks
        a_edge = n % chunks
        j = slot(jnp.where(edge, j_edge, j_inner))
        a = jnp.where(edge, a_edge, a_inner)
        j = jnp.where(first, home, j)
        a = jnp.where(first, i, a)

        @pl.when(jnp.logical_not(first))
        def _():
            w_copy(j, a, forward, 0).wait_recv()

            @pl.when(inner)
            def _():
                @pl.when(j == slot(0))
                def _():
                    w_copy(j, a, forward, 0).start()

                @pl.when(j != slot(0))
                def _():
                    w_copy(j, a, backward, 1).start()

        part[span(a), pl.ds(0, both)] += dot_nt(wts[j, span(a)], tok[j, pl.ds(0, both)])

        @pl.when(a == chunks - 1)
        def _():
            down = wts[j, pl.ds(2 * hid, hid)]
            part[pl.ds(0, hid), pl.ds(both, hid)] += dot_nt(down, down)
            tok[j, pl.ds(both, hid)] = down
            tok[j, pl.ds(both + hid, hid)] = down

    swap = pltpu.make_async_remote_copy(
        src_ref=part,
        dst_ref=part_in,
        send_sem=p_sem.at[0],
        recv_sem=p_sem.at[1],
        device_id=(rep, sibling),
        device_id_type=MESH,
    )
    swap.start()
    swap.wait_recv()
    mine_cols = pl.ds(0, both)
    gram_cols = pl.ds(both, hid)

    def summed(m, c):
        here = pl.ds(m * hid, hid)
        return part[here, c] + part_in[here, c]

    gate = scale_in * summed(0, mine_cols)
    up = scale_in * summed(1, mine_cols)
    sig = jax.nn.sigmoid(gate)
    act = gate * sig
    hidden = (act * up).astype(BF16)
    wwt_hi, wwt_lo = split(summed(0, gram_cols))
    through = dot(wwt_hi, hidden) + dot(wwt_lo, hidden)
    dhidden = (scale_hid / tok_rep) * (summed(2, mine_cols) + scale_hid * through)
    fac[0:hid, 0:both] = (dhidden * up * (sig * (1.0 + gate * (1.0 - sig)))).astype(BF16)
    fac[hid : 2 * hid, 0:both] = (dhidden * act).astype(BF16)
    fac[2 * hid : rows, 0:both] = hidden
    hth_hi, hth_lo = split(scale_hid * dot_nt(hidden, hidden))
    fac[2 * hid : rows, both : both + hid] = hth_hi
    fac[2 * hid : rows, both + hid : both + 2 * hid] = hth_lo

    def gradient(j, a):
        return dot(fac[span(a)], tok[j])

    e_items = [(3 - n // chunks, n % chunks) for n in range(3 * chunks)]
    m_items, late = [], [(0, n) for n in range(chunks)]
    for n in range(2 * chunks):
        m_items.append((3 - n // chunks, n % chunks))
        if n >= 1 and late:
            m_items.append(late.pop(0))

    @each(3 * chunks)
    def _(i):
        j = look(i, [e[0] for e in e_items], [m[0] for m in m_items])
        a = look(i, [e[1] for e in e_items], [m[1] for m in m_items])
        out_going = j > 0
        d = jnp.where(out_going, way, 1 - way)
        to = jnp.where(out_going, forward, backward)
        j = slot(j)

        @pl.when(inner)
        def _():
            g_copy(d, j, a, to).wait_recv()

        acc[d, j, span(a)] = (gradient(j, a) + acc[d, j, span(a)].astype(F32)).astype(BF16)
        g_copy(d, j, a, to).start()

    t = jnp.full((8, 128), step[0].astype(F32) + 1.0, F32)
    fix1 = (1.0 / (1.0 - jnp.exp(t * math.log(0.9))))[0:1, 0:1]
    fix2 = (1.0 / (1.0 - jnp.exp(t * math.log(0.999))))[0:1, 0:1]

    @each(3)
    def _(m):
        for copy in opt_copy(m):
            copy.wait()

    @each(chunks + 1)
    def _(a):
        @pl.when(a < chunks)
        def _():
            g_copy(1 - way, home, a, forward).wait_recv()

            @pl.when(inner)
            def _():
                g_copy(way, home, a, forward).wait_recv()

            g = gradient(home, a) + acc[0, home, span(a)].astype(F32)
            g = g + acc[1, home, span(a)].astype(F32)
            g = g * jnp.where(a < 2 * per, scale_in, scale_hid / tok_rep)
            param = own[span(a)]
            m = (0.9 * mom[span(a)] + 0.1 * g) * fix1
            v = (0.999 * sqr[span(a)] + (0.001 * g) * g) * fix2
            new = param - 0.05 * (m / (jnp.sqrt(v) + 1e-8) + 0.1 * param)
            mine[span(a)] = new.astype(BF16)
            s_copy(a).start()

        @pl.when(a > 0)
        def _():
            b = a - 1
            s_copy(b).wait_recv()
            total = mine[span(b)].astype(F32) + other[span(b)].astype(F32)
            other[span(b)] = (0.5 * total).astype(BF16)
            o_copy(b).start()

    swap.wait_send()

    @each(4)
    def _(j):
        tok_remote(j).wait_send()

    @each(chunks)
    def _(a):
        s_copy(a).wait_send()
        o_copy(a).wait()
        w_copy(home, a, forward, 0).wait_send()
        g_copy(way, slot(3), a, forward).wait_send()
        g_copy(way, slot(2), a, forward).wait_send()

        @pl.when(edge)
        def _():
            g_copy(way, slot(1), a, forward).wait_send()

        @pl.when(inner)
        def _():
            w_copy(slot(0), a, forward, 0).wait_send()
            for j in (1, 2, 3):
                w_copy(slot(j), a, backward, 1).wait_send()
            g_copy(1 - way, slot(0), a, backward).wait_send()


def step_with(bit, tokens, master, moment, square, step):
    near = tokens.shape[1]
    hid, cols = master.shape[2:]
    rows = 3 * hid
    chunks = rows // ROWS
    dma = pltpu.SemaphoreType.DMA
    anywhere = pl.BlockSpec(memory_space=pl.ANY)
    return pl.pallas_call(
        functools.partial(kernel, bit),
        out_shape=jax.ShapeDtypeStruct(master.shape, BF16),
        in_specs=[pl.BlockSpec(memory_space=pltpu.SMEM)] + [anywhere] * 4,
        out_specs=anywhere,
        scratch_shapes=[
            pltpu.VMEM((4, 2 * near + 2 * hid, cols), BF16),
            pltpu.VMEM((4, rows, cols), BF16),
            pltpu.VMEM((2, 4, rows, cols), BF16),
            pltpu.VMEM((rows, cols), F32),
            pltpu.VMEM((rows, cols), F32),
            pltpu.VMEM((rows, cols), F32),
            pltpu.VMEM((rows, 2 * near + 2 * hid), F32),
            pltpu.VMEM((rows, 2 * near + 2 * hid), F32),
            pltpu.VMEM((rows, 2 * near + 2 * hid), BF16),
            pltpu.VMEM((rows, cols), BF16),
            pltpu.VMEM((rows, cols), BF16),
            dma((4,)), dma((4,)), dma((4,)),
            dma((chunks,)), dma((2, 3)),
            dma((2, 4, chunks)), dma((4, chunks)), dma((2,)),
            dma((2, 4, chunks)), dma((2, 4, chunks)),
            dma((chunks,)), dma((chunks,)), dma((chunks,)),
        ],
        compiler_params=pltpu.CompilerParams(
            collective_id=bit, has_side_effects=True, vmem_limit_bytes=40 * 2**20
        ),
        name=f"step_bit{bit}",
    )(step, tokens, master, moment, square)


def per_device(tokens, master, first_moment, second_moment, step_counter):
    bit_count = min(5, lax.axis_size("rep").bit_length() - 1)
    branches = [functools.partial(step_with, bit) for bit in range(bit_count)]
    return lax.switch(
        step_counter[0] % bit_count,
        branches, tokens, master, first_moment, second_moment, step_counter,
    )


def solution(mesh):
    sharded = P("rep", None, None, "fsdp")
    return jax.shard_map(
        per_device,
        mesh=mesh,
        in_specs=(P("rep", "fsdp", None), sharded, sharded, sharded, P()),
        out_specs=sharded,
        check_vma=False,
    )
```

```python
import functools
import math

import jax
import jax.numpy as jnp
from jax import lax
from jax.experimental import pallas as pl
from jax.experimental.pallas import tpu as pltpu
from jax.sharding import PartitionSpec as P

MESH = pl.DeviceIdType.MESH
F32 = jnp.float32
BF16 = jnp.bfloat16
NT = (((1,), (1,)), ((), ()))
CHUNK = 128
LATER = 4
LEAD = 2


def dot(a, b):
    return jnp.dot(a, b, preferred_element_type=F32)


def dot_nt(a, b):
    return lax.dot_general(a, b, NT, preferred_element_type=F32)


def split(x):
    hi = x.astype(BF16)
    return hi, (x - hi.astype(F32)).astype(BF16)


def kernel(
    bit, step, tokens, master, moment, square, out,
    tok, tok_edge, wts, acc, own, mom, sqr, part, part_in, proj, back, back_in, gram, gram_in,
    fac, fac_edge, mine, other,
    tok_sem, tok_send, tok_recv, t_send, t_recv, mas_sem, opt_sem, w_send, w_recv,
    p_sem, b_sem, m_sem, f_sem, g_send, g_recv, s_send, s_recv, o_sem,
):
    rep = lax.axis_index("rep")
    me = lax.axis_index("fsdp")
    chunks, _, hid, _ = own.shape
    cols = chunks * CHUNK
    rows = 3 * hid
    near = tokens.shape[1]
    both = 2 * near
    width = cols * lax.axis_size("fsdp")
    tok_rep = near * lax.axis_size("fsdp")
    scale_in = float(width) ** -0.5
    scale_hid = float(hid) ** -0.5

    home = me // 2
    core = me % 2
    low = home < 2
    edge = jnp.logical_or(home == 0, home == 3)
    inner = jnp.logical_not(edge)
    way = jnp.where(low, 0, 1)
    forward = jnp.where(low, me + 2, me - 2)
    backward = jnp.where(low, me - 2, me + 2)
    sibling = me + 1 - 2 * core
    mate = jnp.where((rep // 2**bit) % 2 == 0, rep + 2**bit, rep - 2**bit)

    def slot(j):
        return jnp.where(low, j, 3 - j)

    barrier = pltpu.get_barrier_semaphore()

    def greet(r, f):
        pl.semaphore_signal(barrier, inc=1, device_id=(r, f), device_id_type=MESH)

    greet(rep, sibling)
    greet(rep, forward)
    greet(mate, me)

    @pl.when(edge)
    def _():
        greet(rep, forward + 1 - 2 * core)

    @pl.when(inner)
    def _():
        greet(rep, backward)
        greet(rep, backward + 1 - 2 * core)

    def remote(src, dst, send, recv, to, r=rep):
        return pltpu.make_async_remote_copy(
            src_ref=src, dst_ref=dst, send_sem=send, recv_sem=recv,
            device_id=(r, to), device_id_type=MESH,
        )

    def columns(f, c):
        return pl.ds(pl.multiple_of(f * cols + c * CHUNK, CHUNK), CHUNK)

    near_rows = pl.ds(pl.multiple_of(core * near, near), near)

    def mas_copy(c):
        return pltpu.make_async_copy(
            master.at[0, :, :, columns(0, c)], own.at[c], mas_sem.at[c]
        )

    def tok_copy(j, c):
        return pltpu.make_async_copy(
            tokens.at[0, :, columns(2 * j + core, c)], tok.at[j, c, near_rows], tok_sem.at[j, c]
        )

    def tok_remote(j, c):
        return remote(
            tokens.at[0, :, columns(2 * j + 1 - core, c)], tok.at[j, c, near_rows],
            tok_send.at[j, c], tok_recv.at[j, c], sibling,
        )

    def t_copy(k, c, source):
        there = pl.ds(pl.multiple_of(source * near, near), near)
        return remote(
            tokens.at[0, :, columns(2 * slot(1) + k, c)], tok_edge.at[c, there],
            t_send.at[k, c], t_recv.at[source, c], 2 * slot(1) + k,
        )

    def w_copy(j, c, to):
        return remote(wts.at[j, c], wts.at[j, c], w_send.at[j, c], w_recv.at[j, c], to)

    def g_copy(d, j, c, to):
        return remote(
            acc.at[d, j, c], acc.at[d, j, c], g_send.at[d, j, c], g_recv.at[d, j, c], to
        )

    def s_copy(c):
        return remote(mine.at[c], other.at[c], s_send.at[c], s_recv.at[c], me, mate)

    def o_copy(c):
        return pltpu.make_async_copy(other.at[c], out.at[0, :, :, columns(0, c)], o_sem.at[c])

    p_copy = remote(part, part_in, p_sem.at[0], p_sem.at[1], sibling)
    b_copy = remote(back, back_in, b_sem.at[0], b_sem.at[1], backward)
    m_copy = remote(gram, gram_in, m_sem.at[0], m_sem.at[1], backward)
    tok_cols = pl.ds(0, both)
    f_copy = remote(
        fac.at[:, tok_cols], fac_edge.at[:, tok_cols], f_sem.at[0], f_sem.at[1], forward
    )
    opt_copies = (
        pltpu.make_async_copy(moment.at[0], mom, opt_sem.at[0]),
        pltpu.make_async_copy(square.at[0], sqr, opt_sem.at[1]),
    )

    def each(count):
        def run(body):
            lax.fori_loop(0, count, lambda i, c: (body(i), c)[1], 0)

        return run

    def used(j):
        return jnp.logical_or(inner, j != slot(1))

    @each(chunks)
    def _(c):
        mas_copy(c).start()

    @each(4 * chunks)
    def _(i):
        j, c = slot(i // chunks), i % chunks

        @pl.when(used(j))
        def _():
            tok_copy(j, c).start()

    for copy in opt_copies:
        copy.start()

    pl.semaphore_wait(barrier, jnp.where(edge, 4, 5))

    @each(chunks)
    def _(c):
        mas_copy(c).wait()
        wts[home, c] = own[c].reshape(rows, CHUNK).astype(BF16)
        w_copy(home, c, forward).start()

    @each(4 * chunks)
    def _(i):
        j, c = (home + i // chunks) % 4, i % chunks

        @pl.when(used(j))
        def _():
            tok_remote(j, c).start()

    @pl.when(edge)
    def _():
        @each(2 * chunks)
        def _(i):
            t_copy(i % 2, i // 2, core).start()

    part[...] = jnp.zeros_like(part)
    proj[...] = jnp.zeros_like(proj)
    for f in (fac, fac_edge):
        f[pl.ds(0, 2 * hid), pl.ds(both, 2 * hid)] = jnp.zeros((2 * hid, 2 * hid), BF16)

    @pl.when(edge)
    def _():
        @each(4)
        def _(j):
            acc[way, j] = jnp.zeros(acc.shape[2:], BF16)

    def project(j, c):
        tok_copy(j, c).wait()
        tok_remote(j, c).wait_recv()
        down = wts[j, c, pl.ds(2 * hid, hid)]
        tok[j, c, pl.ds(both, hid)] = down
        tok[j, c, pl.ds(both + hid, hid)] = down
        part[:, pl.ds(0, both + hid)] += dot_nt(wts[j, c], tok[j, c, pl.ds(0, both + hid)])

    @each(chunks)
    def _(c):
        project(home, c)

    down_rows = pl.ds(2 * hid, hid)
    gram_cols = pl.ds(both, hid)

    @pl.when(inner)
    def _():
        hi, lo = split(part[down_rows, gram_cols])
        gram[:, 0:hid] = hi
        gram[:, hid : 2 * hid] = lo
        m_copy.start()

    @each(2 * chunks)
    def _(n):
        early = n < chunks
        c = n % chunks
        j = slot(jnp.where(early, 2, 3))

        @pl.when(jnp.logical_and(inner, early))
        def _():
            w_copy(slot(0), c, forward).wait_recv()
            w_copy(slot(0), c, forward).start()

        w_copy(j, c, backward).wait_recv()

        @pl.when(inner)
        def _():
            w_copy(j, c, backward).start()

        project(j, c)

        @pl.when(jnp.logical_and(inner, early))
        def _():
            project(slot(0), c)

        @pl.when(jnp.logical_and(inner, jnp.logical_not(early)))
        def _():
            for source in range(2):
                t_copy(core, c, source).wait_recv()
            down = wts[home, c, down_rows]
            tok_edge[c, pl.ds(both, hid)] = down
            tok_edge[c, pl.ds(both + hid, hid)] = down
            proj[...] += dot_nt(wts[home, c], tok_edge[c, pl.ds(0, both)])

    @pl.when(inner)
    def _():
        back[...] = proj[...].astype(BF16)
        b_copy.start()

    @pl.when(edge)
    def _():
        m_copy.wait_recv()
        part[down_rows, gram_cols] += (
            gram_in[:, 0:hid].astype(F32) + gram_in[:, hid : 2 * hid].astype(F32)
        )
        b_copy.wait_recv()
        part[:, tok_cols] += back_in[...].astype(F32)

    p_copy.start()
    p_copy.wait_recv()

    def summed(m, c):
        here = pl.ds(m * hid, hid)
        return part[here, c] + part_in[here, c]

    gate = scale_in * summed(0, tok_cols)
    up = scale_in * summed(1, tok_cols)
    sig = jax.nn.sigmoid(gate)
    act = gate * sig
    hidden = (act * up).astype(BF16)
    wwt_hi, wwt_lo = split(summed(2, gram_cols))
    through = dot(wwt_hi, hidden) + dot(wwt_lo, hidden)
    dhidden = (scale_hid / tok_rep) * (summed(2, tok_cols) + scale_hid * through)
    fac[0:hid, 0:both] = (dhidden * up * (sig * (1.0 + gate * (1.0 - sig)))).astype(BF16)
    fac[hid : 2 * hid, 0:both] = (dhidden * act).astype(BF16)
    fac[2 * hid : rows, 0:both] = hidden

    def moments(f, h):
        hi, lo = split(scale_hid * dot_nt(h, h))
        f[2 * hid : rows, both : both + hid] = hi
        f[2 * hid : rows, both + hid : both + 2 * hid] = lo

    moments(fac, hidden)

    t = jnp.full((8, 128), step[0].astype(F32) + 1.0, F32)
    fix1 = (1.0 / (1.0 - jnp.exp(t * math.log(0.9))))[0:1, 0:1]
    fix2 = (1.0 / (1.0 - jnp.exp(t * math.log(0.999))))[0:1, 0:1]

    for copy in opt_copies:
        copy.wait()

    lag = LEAD + jnp.where(edge, chunks, 1)

    @each(2 * chunks + LEAD + LATER)
    def _(i):
        f = i - lag
        due = jnp.logical_and(f >= 0, f < chunks)

        @each(3)
        def _(q):
            going = q < 2
            c = i - jnp.where(q == 0, 0, jnp.where(going, LEAD, 1))
            j = slot(jnp.where(going, 3 - q, 0))
            d = jnp.where(going, way, 1 - way)
            to = jnp.where(going, forward, backward)

            mine_too = jnp.logical_or(going, inner)

            @pl.when(jnp.logical_and(mine_too, jnp.logical_and(c >= 0, c < chunks)))
            def _():
                @pl.when(inner)
                def _():
                    g_copy(d, j, c, to).wait_recv()

                g = dot(fac[...], tok[j, c])
                acc[d, j, c] = (g + acc[d, j, c].astype(F32)).astype(BF16)
                g_copy(d, j, c, to).start()

        @pl.when(jnp.logical_and(edge, i == 1))
        def _():
            f_copy.start()

        @pl.when(jnp.logical_and(inner, f == 0))
        def _():
            f_copy.wait_recv()
            moments(fac_edge, fac_edge[down_rows, tok_cols])

        @pl.when(due)
        def _():
            proj[:, pl.ds(0, CHUNK)] = dot(fac[...], tok[home, f])

            @pl.when(inner)
            def _():
                proj[:, pl.ds(0, CHUNK)] += dot(fac_edge[...], tok_edge[f])

            g_copy(1 - way, home, f, forward).wait_recv()
            for m in range(3):
                here = pl.ds(m * hid, hid)
                g = proj[here, pl.ds(0, CHUNK)] + acc[1 - way, home, f, here].astype(F32)
                g = g * (scale_in if m < 2 else scale_hid / tok_rep)
                param = own[f, m]
                first = (0.9 * mom[m, :, columns(0, f)] + 0.1 * g) * fix1
                second = (0.999 * sqr[m, :, columns(0, f)] + (0.001 * g) * g) * fix2
                new = param - 0.05 * (first / (jnp.sqrt(second) + 1e-8) + 0.1 * param)
                mine[f, m] = new.astype(BF16)
            s_copy(f).start()

        b = f - LATER

        @pl.when(jnp.logical_and(b >= 0, b < chunks))
        def _():
            s_copy(b).wait_recv()
            other[b] = (0.5 * (mine[b].astype(F32) + other[b].astype(F32))).astype(BF16)
            o_copy(b).start()

    p_copy.wait_send()

    @pl.when(edge)
    def _():
        f_copy.wait_send()

    @pl.when(inner)
    def _():
        m_copy.wait_send()
        b_copy.wait_send()

    @each(4 * chunks)
    def _(i):
        j, c = slot(i // chunks), i % chunks

        @pl.when(used(j))
        def _():
            tok_remote(j, c).wait_send()

        @pl.when(jnp.logical_or(inner, j == home))
        def _():
            w_copy(j, c, forward).wait_send()

    @each(chunks)
    def _(c):
        s_copy(c).wait_send()
        o_copy(c).wait()
        g_copy(way, slot(3), c, forward).wait_send()
        g_copy(way, slot(2), c, forward).wait_send()

        @pl.when(edge)
        def _():
            for k in range(2):
                t_copy(k, c, core).wait_send()

        @pl.when(inner)
        def _():
            g_copy(1 - way, slot(0), c, backward).wait_send()


def step_with(bit, tokens, master, moment, square, step):
    near = tokens.shape[1]
    hid, cols = master.shape[2:]
    rows = 3 * hid
    chunks = cols // CHUNK
    both = 2 * near
    wide = both + 2 * hid
    dma = pltpu.SemaphoreType.DMA
    anywhere = pl.BlockSpec(memory_space=pl.ANY)
    return pl.pallas_call(
        functools.partial(kernel, bit),
        out_shape=jax.ShapeDtypeStruct(master.shape, BF16),
        in_specs=[pl.BlockSpec(memory_space=pltpu.SMEM)] + [anywhere] * 4,
        out_specs=anywhere,
        scratch_shapes=[
            pltpu.VMEM((4, chunks, wide, CHUNK), BF16),
            pltpu.VMEM((chunks, wide, CHUNK), BF16),
            pltpu.VMEM((4, chunks, rows, CHUNK), BF16),
            pltpu.VMEM((2, 4, chunks, rows, CHUNK), BF16),
            pltpu.VMEM((chunks, 3, hid, CHUNK), F32),
            pltpu.VMEM((3, hid, cols), F32),
            pltpu.VMEM((3, hid, cols), F32),
            pltpu.VMEM((rows, wide), F32),
            pltpu.VMEM((rows, wide), F32),
            pltpu.VMEM((rows, both), F32),
            pltpu.VMEM((rows, both), BF16),
            pltpu.VMEM((rows, both), BF16),
            pltpu.VMEM((hid, 2 * hid), BF16),
            pltpu.VMEM((hid, 2 * hid), BF16),
            pltpu.VMEM((rows, wide), BF16),
            pltpu.VMEM((rows, wide), BF16),
            pltpu.VMEM((chunks, 3, hid, CHUNK), BF16),
            pltpu.VMEM((chunks, 3, hid, CHUNK), BF16),
            dma((4, chunks)), dma((4, chunks)), dma((4, chunks)),
            dma((2, chunks)), dma((2, chunks)),
            dma((chunks,)), dma((2,)),
            dma((4, chunks)), dma((4, chunks)),
            dma((2,)), dma((2,)), dma((2,)), dma((2,)),
            dma((2, 4, chunks)), dma((2, 4, chunks)),
            dma((chunks,)), dma((chunks,)), dma((chunks,)),
        ],
        compiler_params=pltpu.CompilerParams(
            collective_id=bit, has_side_effects=True, vmem_limit_bytes=40 * 2**20
        ),
        name=f"step_bit{bit}",
    )(step, tokens, master, moment, square)


def per_device(tokens, master, first_moment, second_moment, step_counter):
    bit_count = min(5, lax.axis_size("rep").bit_length() - 1)
    branches = [functools.partial(step_with, bit) for bit in range(bit_count)]
    return lax.switch(
        step_counter[0] % bit_count,
        branches, tokens, master, first_moment, second_moment, step_counter,
    )


def solution(mesh):
    sharded = P("rep", None, None, "fsdp")
    return jax.shard_map(
        per_device,
        mesh=mesh,
        in_specs=(P("rep", "fsdp", None), sharded, sharded, sharded, P()),
        out_specs=sharded,
        check_vma=False,
    )
```

```python
import functools
import math

import jax
import jax.numpy as jnp
from jax import lax
from jax.experimental import pallas as pl
from jax.experimental.pallas import tpu as pltpu
from jax.sharding import PartitionSpec as P

MESH = pl.DeviceIdType.MESH
F32 = jnp.float32
BF16 = jnp.bfloat16
NT = (((1,), (1,)), ((), ()))
CHUNK = 256
LATER = 3
LEAD = 1


def dot(a, b):
    return jnp.dot(a, b, preferred_element_type=F32)


def dot_nt(a, b):
    return lax.dot_general(a, b, NT, preferred_element_type=F32)


def split(x):
    hi = x.astype(BF16)
    return hi, (x - hi.astype(F32)).astype(BF16)


def kernel(
    bit, step, tokens, master, moment, square, out,
    tok, tok_edge, wts, acc, own, mom, sqr, part, part_in, proj, back, back_in, gram, gram_in,
    fac, fac_edge, mine, other,
    tok_sem, tok_send, tok_recv, t_send, t_recv, mas_sem, opt_sem, w_send, w_recv,
    p_sem, b_sem, m_sem, f_sem, g_send, g_recv, s_send, s_recv, o_sem,
):
    rep = lax.axis_index("rep")
    me = lax.axis_index("fsdp")
    chunks, _, hid, _ = own.shape
    cols = chunks * CHUNK
    rows = 3 * hid
    near = tokens.shape[1]
    both = 2 * near
    width = cols * lax.axis_size("fsdp")
    tok_rep = near * lax.axis_size("fsdp")
    scale_in = float(width) ** -0.5
    scale_hid = float(hid) ** -0.5

    home = me // 2
    core = me % 2
    low = home < 2
    edge = jnp.logical_or(home == 0, home == 3)
    inner = jnp.logical_not(edge)
    way = jnp.where(low, 0, 1)
    forward = jnp.where(low, me + 2, me - 2)
    backward = jnp.where(low, me - 2, me + 2)
    sibling = me + 1 - 2 * core
    mate = jnp.where((rep // 2**bit) % 2 == 0, rep + 2**bit, rep - 2**bit)

    def slot(j):
        return jnp.where(low, j, 3 - j)

    barrier = pltpu.get_barrier_semaphore()

    def greet(r, f):
        pl.semaphore_signal(barrier, inc=1, device_id=(r, f), device_id_type=MESH)

    greet(rep, sibling)
    greet(rep, forward)
    greet(mate, me)

    @pl.when(edge)
    def _():
        greet(rep, forward + 1 - 2 * core)

    @pl.when(inner)
    def _():
        greet(rep, backward)
        greet(rep, backward + 1 - 2 * core)

    def remote(src, dst, send, recv, to, r=rep):
        return pltpu.make_async_remote_copy(
            src_ref=src, dst_ref=dst, send_sem=send, recv_sem=recv,
            device_id=(r, to), device_id_type=MESH,
        )

    def columns(f, c):
        return pl.ds(pl.multiple_of(f * cols + c * CHUNK, CHUNK), CHUNK)

    near_rows = pl.ds(pl.multiple_of(core * near, near), near)

    def mas_copy(c):
        return pltpu.make_async_copy(
            master.at[0, :, :, columns(0, c)], own.at[c], mas_sem.at[c]
        )

    def tok_copy(j, c):
        return pltpu.make_async_copy(
            tokens.at[0, :, columns(2 * j + core, c)], tok.at[j, c, near_rows], tok_sem.at[j, c]
        )

    def tok_remote(j, c):
        return remote(
            tokens.at[0, :, columns(2 * j + 1 - core, c)], tok.at[j, c, near_rows],
            tok_send.at[j, c], tok_recv.at[j, c], sibling,
        )

    def t_copy(k, c, source):
        there = pl.ds(pl.multiple_of(source * near, near), near)
        return remote(
            tokens.at[0, :, columns(2 * slot(1) + k, c)], tok_edge.at[c, there],
            t_send.at[k, c], t_recv.at[source, c], 2 * slot(1) + k,
        )

    def w_copy(j, c, to):
        return remote(wts.at[j, c], wts.at[j, c], w_send.at[j, c], w_recv.at[j, c], to)

    def g_copy(d, j, c, to):
        return remote(
            acc.at[d, j, c], acc.at[d, j, c], g_send.at[d, j, c], g_recv.at[d, j, c], to
        )

    def s_copy(c):
        return remote(mine.at[c], other.at[c], s_send.at[c], s_recv.at[c], me, mate)

    def o_copy(c):
        return pltpu.make_async_copy(other.at[c], out.at[0, :, :, columns(0, c)], o_sem.at[c])

    p_copy = remote(part, part_in, p_sem.at[0], p_sem.at[1], sibling)
    b_copy = remote(back, back_in, b_sem.at[0], b_sem.at[1], backward)
    m_copy = remote(gram, gram_in, m_sem.at[0], m_sem.at[1], backward)
    tok_cols = pl.ds(0, both)
    f_copy = remote(
        fac.at[:, tok_cols], fac_edge.at[:, tok_cols], f_sem.at[0], f_sem.at[1], forward
    )
    opt_copies = (
        pltpu.make_async_copy(moment.at[0], mom, opt_sem.at[0]),
        pltpu.make_async_copy(square.at[0], sqr, opt_sem.at[1]),
    )

    def each(count):
        def run(body):
            lax.fori_loop(0, count, lambda i, c: (body(i), c)[1], 0)

        return run

    def used(j):
        return jnp.logical_or(inner, j != slot(1))

    @each(chunks)
    def _(c):
        mas_copy(c).start()

    @each(4 * chunks)
    def _(i):
        j, c = slot(i // chunks), i % chunks

        @pl.when(used(j))
        def _():
            tok_copy(j, c).start()

    for copy in opt_copies:
        copy.start()

    pl.semaphore_wait(barrier, jnp.where(edge, 4, 5))

    @each(chunks)
    def _(c):
        mas_copy(c).wait()
        wts[home, c] = own[c].reshape(rows, CHUNK).astype(BF16)
        w_copy(home, c, forward).start()

    @each(4 * chunks)
    def _(i):
        j, c = (home + i // chunks) % 4, i % chunks

        @pl.when(used(j))
        def _():
            tok_remote(j, c).start()

    @pl.when(edge)
    def _():
        @each(2 * chunks)
        def _(i):
            t_copy(i % 2, i // 2, core).start()

    part[...] = jnp.zeros_like(part)
    proj[...] = jnp.zeros_like(proj)
    for f in (fac, fac_edge):
        f[pl.ds(0, 2 * hid), pl.ds(both, 2 * hid)] = jnp.zeros((2 * hid, 2 * hid), BF16)

    @pl.when(edge)
    def _():
        @each(4)
        def _(j):
            acc[way, j] = jnp.zeros(acc.shape[2:], BF16)

    def project(j, c):
        tok_copy(j, c).wait()
        tok_remote(j, c).wait_recv()
        down = wts[j, c, pl.ds(2 * hid, hid)]
        tok[j, c, pl.ds(both, hid)] = down
        tok[j, c, pl.ds(both + hid, hid)] = down
        part[:, pl.ds(0, both + hid)] += dot_nt(wts[j, c], tok[j, c, pl.ds(0, both + hid)])

    @each(chunks)
    def _(c):
        project(home, c)

    down_rows = pl.ds(2 * hid, hid)
    gram_cols = pl.ds(both, hid)

    @pl.when(inner)
    def _():
        hi, lo = split(part[down_rows, gram_cols])
        gram[:, 0:hid] = hi
        gram[:, hid : 2 * hid] = lo
        m_copy.start()

    @each(2 * chunks)
    def _(n):
        early = n < chunks
        c = n % chunks
        j = slot(jnp.where(early, 2, 3))

        @pl.when(jnp.logical_and(inner, early))
        def _():
            w_copy(slot(0), c, forward).wait_recv()
            w_copy(slot(0), c, forward).start()

        w_copy(j, c, backward).wait_recv()

        @pl.when(inner)
        def _():
            w_copy(j, c, backward).start()

        project(j, c)

        @pl.when(jnp.logical_and(inner, early))
        def _():
            project(slot(0), c)

        @pl.when(jnp.logical_and(inner, jnp.logical_not(early)))
        def _():
            for source in range(2):
                t_copy(core, c, source).wait_recv()
            down = wts[home, c, down_rows]
            tok_edge[c, pl.ds(both, hid)] = down
            tok_edge[c, pl.ds(both + hid, hid)] = down
            proj[...] += dot_nt(wts[home, c], tok_edge[c, pl.ds(0, both)])

    @pl.when(inner)
    def _():
        back[...] = proj[...].astype(BF16)
        b_copy.start()

    @pl.when(edge)
    def _():
        m_copy.wait_recv()
        part[down_rows, gram_cols] += (
            gram_in[:, 0:hid].astype(F32) + gram_in[:, hid : 2 * hid].astype(F32)
        )
        b_copy.wait_recv()
        part[:, tok_cols] += back_in[...].astype(F32)

    p_copy.start()
    p_copy.wait_recv()

    def summed(m, c):
        here = pl.ds(m * hid, hid)
        return part[here, c] + part_in[here, c]

    gate = scale_in * summed(0, tok_cols)
    up = scale_in * summed(1, tok_cols)
    sig = jax.nn.sigmoid(gate)
    act = gate * sig
    hidden = (act * up).astype(BF16)
    wwt_hi, wwt_lo = split(summed(2, gram_cols))
    through = dot(wwt_hi, hidden) + dot(wwt_lo, hidden)
    dhidden = (scale_hid / tok_rep) * (summed(2, tok_cols) + scale_hid * through)
    fac[0:hid, 0:both] = (dhidden * up * (sig * (1.0 + gate * (1.0 - sig)))).astype(BF16)
    fac[hid : 2 * hid, 0:both] = (dhidden * act).astype(BF16)
    fac[2 * hid : rows, 0:both] = hidden

    def moments(f, h):
        hi, lo = split(scale_hid * dot_nt(h, h))
        f[2 * hid : rows, both : both + hid] = hi
        f[2 * hid : rows, both + hid : both + 2 * hid] = lo

    moments(fac, hidden)

    t = jnp.full((8, 128), step[0].astype(F32) + 1.0, F32)
    fix1 = (1.0 / (1.0 - jnp.exp(t * math.log(0.9))))[0:1, 0:1]
    fix2 = (1.0 / (1.0 - jnp.exp(t * math.log(0.999))))[0:1, 0:1]

    for copy in opt_copies:
        copy.wait()

    lag = LEAD + jnp.where(edge, chunks, 1)

    @each(2 * chunks + LEAD + LATER)
    def _(i):
        f = i - lag
        due = jnp.logical_and(f >= 0, f < chunks)

        @each(3)
        def _(q):
            going = q < 2
            c = i - jnp.where(q == 0, 0, jnp.where(going, LEAD, 1))
            j = slot(jnp.where(going, 3 - q, 0))
            d = jnp.where(going, way, 1 - way)
            to = jnp.where(going, forward, backward)

            mine_too = jnp.logical_or(going, inner)

            @pl.when(jnp.logical_and(mine_too, jnp.logical_and(c >= 0, c < chunks)))
            def _():
                @pl.when(inner)
                def _():
                    g_copy(d, j, c, to).wait_recv()

                g = dot(fac[...], tok[j, c])
                acc[d, j, c] = (g + acc[d, j, c].astype(F32)).astype(BF16)
                g_copy(d, j, c, to).start()

        @pl.when(jnp.logical_and(edge, i == 1))
        def _():
            f_copy.start()

        @pl.when(jnp.logical_and(inner, f == 0))
        def _():
            f_copy.wait_recv()
            moments(fac_edge, fac_edge[down_rows, tok_cols])

        @pl.when(due)
        def _():
            proj[:, pl.ds(0, CHUNK)] = dot(fac[...], tok[home, f])

            @pl.when(inner)
            def _():
                proj[:, pl.ds(0, CHUNK)] += dot(fac_edge[...], tok_edge[f])

            g_copy(1 - way, home, f, forward).wait_recv()
            for m in range(3):
                here = pl.ds(m * hid, hid)
                g = proj[here, pl.ds(0, CHUNK)] + acc[1 - way, home, f, here].astype(F32)
                g = g * (scale_in if m < 2 else scale_hid / tok_rep)
                param = own[f, m]
                first = (0.9 * mom[m, :, columns(0, f)] + 0.1 * g) * fix1
                second = (0.999 * sqr[m, :, columns(0, f)] + (0.001 * g) * g) * fix2
                new = param - 0.05 * (first / (jnp.sqrt(second) + 1e-8) + 0.1 * param)
                mine[f, m] = new.astype(BF16)
            s_copy(f).start()

        b = f - LATER

        @pl.when(jnp.logical_and(b >= 0, b < chunks))
        def _():
            s_copy(b).wait_recv()
            other[b] = (0.5 * (mine[b].astype(F32) + other[b].astype(F32))).astype(BF16)
            o_copy(b).start()

    p_copy.wait_send()

    @pl.when(edge)
    def _():
        f_copy.wait_send()

    @pl.when(inner)
    def _():
        m_copy.wait_send()
        b_copy.wait_send()

    @each(4 * chunks)
    def _(i):
        j, c = slot(i // chunks), i % chunks

        @pl.when(used(j))
        def _():
            tok_remote(j, c).wait_send()

        @pl.when(jnp.logical_or(inner, j == home))
        def _():
            w_copy(j, c, forward).wait_send()

    @each(chunks)
    def _(c):
        s_copy(c).wait_send()
        o_copy(c).wait()
        g_copy(way, slot(3), c, forward).wait_send()
        g_copy(way, slot(2), c, forward).wait_send()

        @pl.when(edge)
        def _():
            for k in range(2):
                t_copy(k, c, core).wait_send()

        @pl.when(inner)
        def _():
            g_copy(1 - way, slot(0), c, backward).wait_send()


def step_with(bit, tokens, master, moment, square, step):
    near = tokens.shape[1]
    hid, cols = master.shape[2:]
    rows = 3 * hid
    chunks = cols // CHUNK
    both = 2 * near
    wide = both + 2 * hid
    dma = pltpu.SemaphoreType.DMA
    anywhere = pl.BlockSpec(memory_space=pl.ANY)
    return pl.pallas_call(
        functools.partial(kernel, bit),
        out_shape=jax.ShapeDtypeStruct(master.shape, BF16),
        in_specs=[pl.BlockSpec(memory_space=pltpu.SMEM)] + [anywhere] * 4,
        out_specs=anywhere,
        scratch_shapes=[
            pltpu.VMEM((4, chunks, wide, CHUNK), BF16),
            pltpu.VMEM((chunks, wide, CHUNK), BF16),
            pltpu.VMEM((4, chunks, rows, CHUNK), BF16),
            pltpu.VMEM((2, 4, chunks, rows, CHUNK), BF16),
            pltpu.VMEM((chunks, 3, hid, CHUNK), F32),
            pltpu.VMEM((3, hid, cols), F32),
            pltpu.VMEM((3, hid, cols), F32),
            pltpu.VMEM((rows, wide), F32),
            pltpu.VMEM((rows, wide), F32),
            pltpu.VMEM((rows, both), F32),
            pltpu.VMEM((rows, both), BF16),
            pltpu.VMEM((rows, both), BF16),
            pltpu.VMEM((hid, 2 * hid), BF16),
            pltpu.VMEM((hid, 2 * hid), BF16),
            pltpu.VMEM((rows, wide), BF16),
            pltpu.VMEM((rows, wide), BF16),
            pltpu.VMEM((chunks, 3, hid, CHUNK), BF16),
            pltpu.VMEM((chunks, 3, hid, CHUNK), BF16),
            dma((4, chunks)), dma((4, chunks)), dma((4, chunks)),
            dma((2, chunks)), dma((2, chunks)),
            dma((chunks,)), dma((2,)),
            dma((4, chunks)), dma((4, chunks)),
            dma((2,)), dma((2,)), dma((2,)), dma((2,)),
            dma((2, 4, chunks)), dma((2, 4, chunks)),
            dma((chunks,)), dma((chunks,)), dma((chunks,)),
        ],
        compiler_params=pltpu.CompilerParams(
            collective_id=bit, has_side_effects=True, vmem_limit_bytes=40 * 2**20
        ),
        name=f"step_bit{bit}",
    )(step, tokens, master, moment, square)


def per_device(tokens, master, first_moment, second_moment, step_counter):
    bit_count = min(5, lax.axis_size("rep").bit_length() - 1)
    branches = [functools.partial(step_with, bit) for bit in range(bit_count)]
    return lax.switch(
        step_counter[0] % bit_count,
        branches, tokens, master, first_moment, second_moment, step_counter,
    )


def solution(mesh):
    sharded = P("rep", None, None, "fsdp")
    return jax.shard_map(
        per_device,
        mesh=mesh,
        in_specs=(P("rep", "fsdp", None), sharded, sharded, sharded, P()),
        out_specs=sharded,
        check_vma=False,
    )
```
